32 devices in a mesh: branch: 4 (over z), vocab: 8 (over y, x, core).
Axes of the slice: x: 2, y: 2, z: 4, core: 2. Of those that a mesh axis runs over, the one named last changes fastest.
Arguments:
- teacher_hidden: bfloat16 [4, 768, 4096], P('branch', None, 'vocab'), may hold values from -300 to 300
- teacher_weight: bfloat16 [4, 4096, 32000], P('branch', None, 'vocab'), may hold values from -0.375 to 0.375
- student_hidden: bfloat16 [768, 4096], P('branch', 'vocab'), may hold values from -300 to 300
- student_weight: bfloat16 [4096, 32000], P(None, 'vocab'), may hold values from -0.375 to 0.375
- branch_weight: float32 [4], replicated, may hold values from 0.2 to 5
- assignment: int32 [4], replicated, may hold values from 0 to 3, each once
- targets: int32 [768], P('branch'), may hold values from 0 to 31999
Outputs:
- divergence: float32 [768], P('branch')
- target_loss: float32 [768], P('branch')
The draws below stay inside these ranges and needn't reach their ends.
Inputs may be any that keep to these rules, and one draw needn't show every extreme that they name: `assignment`: each branch number appears once.
All inputs are finite; a program needn't handle non-finite values.
Results may differ from the reference program's by a relative error of at most 0.0003.
Values may be sent and summed in bfloat16 or wider, within the bound.
A program may use at most 192 MiB of HBM per device.

```python
import math
import jax
import jax.numpy as jnp

D = 4096
V = 32000
BRANCHES = 4
TOKENS = 768


def hidden_states(key, shape, plain_low, plain_high):
    first, second = jax.random.split(key)
    values = jax.random.normal(first, shape, jnp.float32)
    scales = jnp.exp(jax.random.uniform(second, shape[:-1] + (1,), jnp.float32, jnp.log(plain_low), jnp.log(plain_high)))
    values = values * scales
    return jnp.clip(values, -300.0, 300.0)


def draw_teacher_hidden(key, part):
    return hidden_states(jax.random.fold_in(key, 11), (BRANCHES, TOKENS, D), 0.4, 1.2).astype(jnp.bfloat16)


def draw_student_hidden(key, part):
    return hidden_states(jax.random.fold_in(key, 23), (TOKENS, D), 1.0, 1.0).astype(jnp.bfloat16)


def plant(entries, rng, smallest, high):
    extent = entries.shape
    spot = [jax.random.randint(jax.random.fold_in(rng, axis), (), 0, extent[axis]) for axis in range(len(extent))]
    entries = entries.at[tuple(spot)].set(smallest)
    longest = extent.index(max(extent))
    spot[longest] = (spot[longest] + 1) % extent[longest]
    return entries.at[tuple(spot)].set(high)


def block_levels(own_key, dims, shards, smallest, high):
    loudness = 1.0
    for dim, shards_of in shards:
        heights = jax.random.uniform(jax.random.fold_in(jax.random.fold_in(own_key, 6), dim), (shards_of,), jnp.float32, smallest / len(shards), high / len(shards))
        loudness = loudness * jnp.repeat(jnp.exp(heights), dims[dim] // shards_of).reshape((-1,) + (1,) * (len(dims) - 1 - dim))
    return loudness


def gaussian(key, extent, scale, limit, cuts=(), held_as=jnp.bfloat16):
    drawn = scale * jax.random.normal(key, extent, jnp.float32)
    if cuts:
        drawn = drawn * block_levels(key, extent, cuts, -0.22, 0.18)
    return jnp.clip(drawn, -limit, limit).astype(held_as)


def setup_inputs(seed: int = 0) -> dict:
    splits = jax.random.split(jax.random.key(seed), 8)
    return {
        "teacher_hidden": draw_teacher_hidden(jax.random.fold_in(splits[7], 71), 0),
        "teacher_weight": gaussian(splits[1], (BRANCHES, D, V), (D // 16) ** -0.5, 0.375, ((0, 4), (2, 8))),
        "student_hidden": draw_student_hidden(jax.random.fold_in(splits[7], 71), 0),
        "student_weight": gaussian(splits[3], (D, V), (D // 16) ** -0.5, 0.375, ((1, 8),)),
        "branch_weight": jnp.clip(jnp.exp(jax.random.uniform(splits[4], (BRANCHES,), jnp.float32, math.log(0.2), math.log(5.0))), 0.2, 5.0),
        "assignment": jax.random.permutation(splits[5], BRANCHES).astype(jnp.int32),
        "targets": plant(jax.random.randint(splits[6], (TOKENS,), 0, V), jax.random.fold_in(splits[6], 1), 0, V - 1).astype(jnp.int32),
    }


def log_total(logits):
    highest = jnp.max(logits, axis=-1, keepdims=True)
    return highest[..., 0] + jnp.log(jnp.sum(jnp.exp(logits - highest), axis=-1))


def reference(teacher_hidden, teacher_weight, student_hidden, student_weight, branch_weight, assignment, targets):
    share = branch_weight / jnp.sum(branch_weight)
    log_share = jnp.log(share)[assignment]
    stacked = []
    for group in range(BRANCHES):
        logits = jnp.dot(teacher_hidden[group], teacher_weight[group], preferred_element_type=jnp.float32)
        stacked.append(logits - log_total(logits)[:, None] + log_share[group])
    stacked = jnp.stack(stacked, axis=0)
    highest = jnp.max(stacked, axis=0)
    mixture = highest + jnp.log(jnp.sum(jnp.exp(stacked - highest[None]), axis=0))
    student_logits = jnp.dot(student_hidden, student_weight, preferred_element_type=jnp.float32)
    log_student = student_logits - log_total(student_logits)[:, None]
    divergence = jnp.sum(jnp.exp(mixture) * (mixture - log_student), axis=1)
    picked = jnp.take_along_axis(log_student, targets[:, None].astype(jnp.int32), axis=1)[:, 0]
    return divergence, -picked
```

```python
import jax
import jax.numpy as jnp
from jax import lax
from jax.sharding import PartitionSpec as P

CHUNKS = 6
SCALE = 2.0**30


def encode(p):
    p = p * SCALE
    p = p * p
    return (p * p).astype(jnp.bfloat16)


def decode(code):
    return lax.rsqrt(lax.rsqrt(code.astype(jnp.float32))) * (1.0 / SCALE)


def add_product(piece, weights):
    return jnp.dot(piece, weights, preferred_element_type=jnp.float32)


def max_and_sum(logits):
    top = jnp.max(logits, axis=1)
    return top, jnp.sum(jnp.exp(logits - top[:, None]), axis=1)


def merge_lse(tops, sums):
    top = jnp.max(tops, axis=0)
    return top + jnp.log(jnp.sum(sums * jnp.exp(tops - top[None]), axis=0))


def per_device(
    teacher_hidden,
    teacher_weight,
    student_hidden,
    student_weight,
    branch_weight,
    assignment,
    targets,
):
    weights = teacher_weight[0]
    width = weights.shape[1]
    group = lax.axis_index("branch")
    n = lax.axis_size("branch")
    half_n = n // 2
    tokens = teacher_hidden.shape[1]
    half = tokens // 2
    rows = half // CHUNKS
    share = branch_weight / jnp.sum(branch_weight)
    log_share = jnp.log(share)[assignment]
    own_share = jnp.sum(jnp.where(jnp.arange(n) == group, log_share, 0.0))

    hidden = lax.all_gather(teacher_hidden[0], "vocab", axis=1, tiled=True)
    groups = [list(range(half_n)), list(range(half_n, n))]
    student = lax.all_gather(student_hidden, "branch", axis=0, tiled=True, axis_index_groups=groups)
    picks = lax.all_gather(targets, "branch", axis=0, tiled=True, axis_index_groups=groups)
    student = lax.all_gather(student, "vocab", axis=1, tiled=True)

    logits = add_product(hidden, weights)
    top, total = max_and_sum(logits)
    parts = lax.all_gather(jnp.stack([top, total]), "vocab", axis=0)
    lse = merge_lse(parts[:, 0], parts[:, 1])
    offset = own_share - lse

    student_logits = add_product(student, student_weight)

    def own(first, chunk):
        start = first + jnp.clip(chunk, 0, CHUNKS - 1) * rows
        piece = lax.dynamic_slice(logits, (start, 0), (rows, width))
        return jnp.exp(piece + lax.dynamic_slice(offset, (start,), (rows,))[:, None])

    up = [(i, i + 1) for i in range(n - 1)]
    down = [(i + 1, i) for i in range(n - 1)]
    from_left = jnp.zeros((rows, width), jnp.bfloat16)
    from_right = from_left
    last = group == n - 1
    ends = []
    for step in range(CHUNKS + n - 1):
        up_sum = own(half, step - group) + decode(from_left)
        down_sum = own(0, step - (n - 1 - group)) + decode(from_right)
        if step >= n - 1:
            ends.append(jnp.where(last, up_sum, down_sum))
        if step < CHUNKS + n - 2:
            from_left = lax.ppermute(encode(up_sum), "branch", up)
            from_right = lax.ppermute(encode(down_sum), "branch", down)
    q = jnp.concatenate(ends, axis=0)
    mixture = jnp.log(jnp.maximum(q, 1e-37))
    s_top, s_total = max_and_sum(student_logits)
    shifted = student_logits - s_top[:, None]
    columns = lax.axis_index("vocab") * width + jnp.arange(width, dtype=jnp.int32)
    matches = columns[None, :] == picks[:, None]
    hit = jnp.sum(jnp.where(matches, student_logits, 0.0), axis=1)
    cross = jnp.sum(q * (mixture - shifted), axis=1)
    mass = jnp.sum(q, axis=1)
    parts = lax.all_gather(jnp.stack([s_top, s_total, hit, cross, mass]), "vocab", axis=0)
    s_lse = merge_lse(parts[:, 0], parts[:, 1])
    loss = s_lse - jnp.sum(parts[:, 2], axis=0)
    mass = jnp.sum(parts[:, 4], axis=0)
    cross = jnp.sum(parts[:, 3] + parts[:, 4] * (s_lse[None] - parts[:, 0]), axis=0)
    divergence = cross / mass - jnp.log(mass)
    both = lax.all_gather(jnp.stack([divergence, loss]), "branch", axis=0)
    mine = jnp.where(group < half_n, both[0], both[n - 1])
    per = tokens // n
    mine = lax.dynamic_slice(mine, (0, (group % half_n) * per), (2, per))
    return mine[0], mine[1]


def solution(mesh):
    in_specs = (
        P("branch", None, "vocab"),
        P("branch", None, "vocab"),
        P("branch", "vocab"),
        P(None, "vocab"),
        P(),
        P(),
        P("branch"),
    )
    out_specs = (P("branch"), P("branch"))
    return jax.shard_map(
        per_device, mesh=mesh, in_specs=in_specs, out_specs=out_specs, check_vma=False
    )
```

```python
import functools

import jax
import jax.numpy as jnp
from jax import lax
from jax.experimental import pallas as pl
from jax.experimental.pallas import tpu as pltpu
from jax.sharding import PartitionSpec as P

MESH = pl.DeviceIdType.MESH
SCALE = 2.0**30
LOG_SCALE = 20.79441541679836
PIECES = 32
BLOCK = 80
TILE = 800
SLOTS = 3
LAG = 2


def divisor(width, most):
    return max(t for t in range(8, most + 1, 8) if width % t == 0)


def piece_rows(width):
    return min(t for t in range(8, width + 1, 8) if width % t == 0 and width // t <= PIECES)


def flip(chip, e, chips):
    out, bit = 0, 1
    while bit < chips:
        out = out + bit * ((chip // bit + e // bit) % 2)
        bit *= 2
    return out


def kernel(
    n, nv, hidden, weight, student, s_weight, branch_weight, assignment, targets, out,
    hid, shid, wbuf, acc, sacc, up_in, down_in, up_out, down_out, factor, rows_in, fin_in, tbuf, res,
    local_sem, w_sem, h_send, h_recv, s_send, s_recv, p_send, p_recv, t_send, t_recv,
    up_send, up_recv, down_send, down_recv, l_send, l_recv, f_send, f_recv, r_send, r_recv,
):
    z, v = lax.axis_index("branch"), lax.axis_index("vocab")
    chips = nv // 2
    chip, core = v // 2, v % 2
    sibling = v + 1 - 2 * core
    half_n = n // 2
    tokens, feat = hid.shape[1], hid.shape[2]
    half, per, width = tokens // 2, tokens // n, acc.shape[0]
    rows_each = piece_rows(width)
    pieces = width // rows_each
    block, tile_rows = divisor(width, BLOCK), divisor(width, TILE)
    upper = z // half_n
    end = upper * (n - 1)
    is_end = z == end
    place = z % half_n

    def remote(src, dst, send, recv, zz, vv):
        return pltpu.make_async_remote_copy(
            src_ref=src, dst_ref=dst, send_sem=send, recv_sem=recv, device_id=(zz, vv), device_id_type=MESH
        )

    def owner(s):
        return flip(chip, s // 2, chips) * 2 + (core + s) % 2

    def fetch(src, s):
        slot = s % SLOTS
        features = pl.ds(pl.multiple_of(owner(s) * feat, feat), feat)
        return pltpu.make_async_copy(src.at[:, features], wbuf.at[slot], w_sem.at[slot])

    t_weight = weight.at[0]
    own = pltpu.make_async_copy(hidden.at[0], hid.at[0], local_sem.at[0])
    own.start()
    mine = pl.ds(pl.multiple_of(place * per, per), per)
    own_student = pltpu.make_async_copy(student, shid.at[0, mine], local_sem.at[1])
    own_targets = pltpu.make_async_copy(targets, tbuf.at[place], local_sem.at[2])

    @pl.when(is_end)
    def _():
        own_student.start()
        own_targets.start()

    fetch(t_weight, 0).start()
    fetch(t_weight, 1).start()

    barrier = pltpu.get_barrier_semaphore()
    for d in range(1, nv):
        pl.semaphore_signal(barrier, inc=1, device_id=(z, (v + d) % nv), device_id_type=MESH)
    for d in range(1, n):
        pl.semaphore_signal(barrier, inc=1, device_id=((z + d) % n, v), device_id_type=MESH)
    own.wait()
    pl.semaphore_wait(barrier, nv - 1 + n - 1)

    def push(buf, send, recv, e):
        return remote(buf.at[0], buf.at[2 * e], send.at[2 * e], recv.at[2 * e], z, flip(chip, e, chips) * 2 + core)

    def forward(buf, send, recv, e):
        return remote(buf.at[2 * e], buf.at[2 * e + 1], send.at[2 * e + 1], recv.at[2 * e + 1], z, sibling)

    def begin(buf, send, recv):
        forward(buf, send, recv, 0).start()
        for e in range(1, min(3, chips)):
            push(buf, send, recv, e).start()

    def chunk_step(s, buf, send, recv, src, total):
        @pl.when(s + 2 < nv)
        def _():
            fetch(src, s + 2).start()

        e = s // 2

        @pl.when((s % 2 == 0) & (s > 0))
        def _():
            push(buf, send, recv, e).wait_recv()
            forward(buf, send, recv, e).start()

            @pl.when(e + 2 < chips)
            def _():
                push(buf, send, recv, e + 2).start()

        @pl.when(s % 2 == 1)
        def _():
            forward(buf, send, recv, e).wait_recv()

        fetch(src, s).wait()
        slot = s % SLOTS

        @pl.loop(0, width // tile_rows)
        def _(j):
            rows = pl.ds(pl.multiple_of(j * tile_rows, tile_rows), tile_rows)
            total[rows, :] += lax.dot_general(
                wbuf[slot, rows, :], buf[s], (((1,), (1,)), ((), ())), preferred_element_type=jnp.float32
            )

    def finish_sends(buf, send, recv):
        @pl.loop(0, chips)
        def _(e):
            forward(buf, send, recv, e).wait_send()

        @pl.loop(1, chips)
        def _(e):
            push(buf, send, recv, e).wait_send()

    begin(hid, h_send, h_recv)

    pass_student = remote(student, shid.at[0, mine], p_send, p_recv.at[place], end, v)
    pass_targets = remote(targets, tbuf.at[place], t_send, t_recv.at[place], end, v)

    @pl.when(z != end)
    def _():
        pass_student.start()
        pass_targets.start()

    def block_rows(i):
        return pl.ds(pl.multiple_of(i * block, block), block)

    @pl.loop(0, width // block)
    def _(i):
        acc[block_rows(i), :] = jnp.zeros((block, tokens), jnp.float32)

    @pl.loop(0, nv)
    def _(s):
        chunk_step(s, hid, h_send, h_recv, t_weight, acc)

    @pl.when(is_end)
    def _():
        fetch(s_weight, 0).start()
        fetch(s_weight, 1).start()
        own_student.wait()
        own_targets.wait()

        @pl.loop(0, half_n)
        def _(j):
            @pl.when(j != place)
            def _():
                there = pl.ds(pl.multiple_of(j * per, per), per)
                remote(student, shid.at[0, there], p_send, p_recv.at[j], z, v).wait_recv()
                remote(targets, tbuf.at[j], t_send, t_recv.at[j], z, v).wait_recv()

        begin(shid, s_send, s_recv)

        @pl.loop(0, width // block)
        def _(i):
            sacc[block_rows(i), :] = jnp.zeros((block, half), jnp.float32)

    def fold(x, reduce):
        return reduce(x.reshape(block // 8, 8, x.shape[1]), axis=0)

    def highest(logits):
        low = jnp.full((8, logits.shape[1]), -jnp.inf, jnp.float32)
        top = lax.fori_loop(
            0, width // block, lambda i, top: jnp.maximum(top, fold(logits[block_rows(i), :], jnp.max)), low
        )
        return jnp.max(top, axis=0, keepdims=True)

    def rows_of(*values):
        row = lax.broadcasted_iota(jnp.int32, (8, values[0].shape[1]), 0)
        packed = jnp.zeros(row.shape, jnp.float32)
        for i, value in enumerate(values):
            packed = jnp.where(row == i, value, packed)
        return packed

    top = highest(acc)

    def exponentials(i, total):
        x = jnp.exp(acc[block_rows(i), :] - top)
        acc[block_rows(i), :] = x
        return total + fold(x, jnp.sum)

    total = lax.fori_loop(0, width // block, exponentials, jnp.zeros((8, tokens), jnp.float32))
    rows_in[0] = rows_of(top, jnp.sum(total, axis=0, keepdims=True))

    def exchange(buf, send, recv):
        @pl.loop(1, nv)
        def _(d):
            remote(buf.at[0], buf.at[d], send.at[d], recv.at[d], z, (v + d) % nv).start()

        @pl.loop(1, nv)
        def _(d):
            remote(buf.at[0], buf.at[d], send.at[d], recv.at[d], z, (v + d) % nv).wait()

    def merge(buf):
        top = buf[0, 0:1, :]
        for d in range(1, nv):
            top = jnp.maximum(top, buf[d, 0:1, :])
        total = jnp.zeros_like(top)
        for d in range(nv):
            total += buf[d, 1:2, :] * jnp.exp(buf[d, 0:1, :] - top)
        return top + jnp.log(total)

    exchange(rows_in, l_send, l_recv)
    weights = branch_weight[...]
    log_share = jnp.log(weights / jnp.sum(weights, axis=1, keepdims=True))
    index = lax.broadcasted_iota(jnp.int32, weights.shape, 1)
    chosen = jnp.sum(
        jnp.where(index == z, assignment[...].astype(jnp.float32), 0.0), axis=1, keepdims=True
    )
    own_share = jnp.sum(
        jnp.where(index.astype(jnp.float32) == chosen, log_share, 0.0), axis=1, keepdims=True
    )
    scale = jnp.exp(rows_in[0, 0:1, :] - merge(rows_in) + own_share) * SCALE
    factor[...] = jnp.broadcast_to(scale, (8, tokens))

    def piece_up(c):
        return remote(up_out.at[c], up_in.at[c], up_send.at[c], up_recv.at[c], lax.rem(z + 1, n), v)

    def piece_down(c):
        return remote(down_out.at[c], down_in.at[c], down_send.at[c], down_recv.at[c], lax.rem(z + n - 1, n), v)

    def turn(c, base, order, piece, came, leaves):
        rows = pl.ds(pl.multiple_of(c * rows_each, rows_each), rows_each)
        lanes = pl.ds(base, half)

        @pl.when(order == 0)
        def _():
            p = acc[rows, lanes] * factor[:1, lanes]
            p = p * p
            leaves[c] = (p * p).astype(jnp.bfloat16)
            piece(c).start()

        @pl.when(order > 0)
        def _():
            piece(c).wait_recv()
            p = acc[rows, lanes] * factor[:1, lanes] + lax.rsqrt(lax.rsqrt(came[c].astype(jnp.float32)))

            @pl.when(order < n - 1)
            def _():
                square = p * p
                leaves[c] = (square * square).astype(jnp.bfloat16)
                piece(c).start()

            @pl.when(order == n - 1)
            def _():
                acc[rows, lanes] = p

    first_student = LAG * (n - 1) - 2

    @pl.loop(0, max(pieces + LAG * (n - 1), first_student + nv))
    def _(k):
        c = k - LAG * z

        @pl.when((c >= 0) & (c < pieces))
        def _():
            turn(c, half, z, piece_up, up_in, up_out)

        o = n - 1 - z
        d = k - LAG * o

        @pl.when((d >= 0) & (d < pieces))
        def _():
            turn(d, 0, o, piece_down, down_in, down_out)

        s = k - first_student

        @pl.when(is_end & (s >= 0) & (s < nv))
        def _():
            chunk_step(s, shid, s_send, s_recv, s_weight, sacc)

    @pl.when(is_end)
    def _():
        lanes = pl.ds(pl.multiple_of(upper * half, half), half)
        s_top = highest(sacc)
        picks = tbuf[0]
        for j in range(1, half_n):
            picks = picks + tbuf[j]
        picks = picks[:1] - v * width
        vocab_row = lax.broadcasted_iota(jnp.int32, (block, half), 0)

        def terms(i, sums):
            x = sacc[block_rows(i), :]
            q = acc[block_rows(i), lanes]
            hit = jnp.where(vocab_row + i * block == picks, x, 0.0)
            x = x - s_top
            mixture = jnp.log(jnp.maximum(q, 1e-30)) - LOG_SCALE
            q = q * (1.0 / SCALE)
            new = (jnp.exp(x), hit, q * (mixture - x), q)
            return tuple(old + fold(value, jnp.sum) for old, value in zip(sums, new))

        sums = lax.fori_loop(0, width // block, terms, (jnp.zeros((8, half), jnp.float32),) * 4)
        fin_in[0] = rows_of(s_top, *(jnp.sum(value, axis=0, keepdims=True) for value in sums))
        exchange(fin_in, f_send, f_recv)
        lse = merge(fin_in)
        hit, cross, mass = (jnp.zeros((1, half), jnp.float32) for _ in range(3))
        for d in range(nv):
            hit += fin_in[d, 2:3, :]
            mass += fin_in[d, 4:5, :]
            cross += fin_in[d, 3:4, :] + fin_in[d, 4:5, :] * (lse - fin_in[d, 0:1, :])
        row = lax.broadcasted_iota(jnp.int32, (8, half), 0)
        res[...] = jnp.where(row == 0, cross / mass - jnp.log(mass), lse - hit)

        def give(j):
            return remote(res, res, r_send.at[j], r_recv, upper * half_n + j, v)

        for act in ("start", "wait_send"):
            @pl.loop(0, half_n)
            def _(j):
                @pl.when(j != place)
                def _():
                    getattr(give(j), act)()

        finish_sends(shid, s_send, s_recv)

    @pl.when(z != end)
    def _():
        remote(res, res, r_send.at[0], r_recv, end, v).wait_recv()
        pass_student.wait_send()
        pass_targets.wait_send()

    out[...] = res[...]
    finish_sends(hid, h_send, h_recv)

    @pl.loop(0, pieces)
    def _(c):
        @pl.when(z < n - 1)
        def _():
            piece_up(c).wait_send()

        @pl.when(z > 0)
        def _():
            piece_down(c).wait_send()


def per_device(
    teacher_hidden,
    teacher_weight,
    student_hidden,
    student_weight,
    branch_weight,
    assignment,
    targets,
):
    n, nv = lax.axis_size("branch"), lax.axis_size("vocab")
    _, tokens, feat = teacher_hidden.shape
    width = teacher_weight.shape[2]
    half, per = tokens // 2, tokens // n
    rows_each = piece_rows(width)
    pieces = width // rows_each
    first = lax.axis_index("branch") % (n // 2) * per
    spread = jnp.zeros((8, half), jnp.int32)
    spread = lax.dynamic_update_slice(spread, jnp.broadcast_to(targets[None], (8, per)), (0, first))
    f32, bf16 = jnp.float32, jnp.bfloat16
    dma = pltpu.SemaphoreType.DMA
    anywhere = pl.BlockSpec(memory_space=pl.ANY)
    vmem = pl.BlockSpec(memory_space=pltpu.VMEM)
    result = pl.pallas_call(
        functools.partial(kernel, n, nv),
        out_shape=jax.ShapeDtypeStruct((8, half), f32),
        in_specs=[anywhere, anywhere, anywhere, anywhere, vmem, vmem, vmem],
        out_specs=vmem,
        scratch_shapes=[
            pltpu.VMEM((nv, tokens, feat), bf16),
            pltpu.VMEM((nv, half, feat), bf16),
            pltpu.VMEM((SLOTS, width, feat), bf16),
            pltpu.VMEM((width, tokens), f32),
            pltpu.VMEM((width, half), f32),
            pltpu.VMEM((pieces, rows_each, half), bf16),
            pltpu.VMEM((pieces, rows_each, half), bf16),
            pltpu.VMEM((pieces, rows_each, half), bf16),
            pltpu.VMEM((pieces, rows_each, half), bf16),
            pltpu.VMEM((8, tokens), f32),
            pltpu.VMEM((nv, 8, tokens), f32),
            pltpu.VMEM((nv, 8, half), f32),
            pltpu.VMEM((n // 2, 8, half), jnp.int32),
            pltpu.VMEM((8, half), f32),
            dma((3,)),
            dma((SLOTS,)),
            dma((nv,)), dma((nv,)),
            dma((nv,)), dma((nv,)),
            dma, dma((n // 2,)),
            dma, dma((n // 2,)),
            dma((pieces,)), dma((pieces,)),
            dma((pieces,)), dma((pieces,)),
            dma((nv,)), dma((nv,)),
            dma((nv,)), dma((nv,)),
            dma((n // 2,)), dma,
        ],
        compiler_params=pltpu.CompilerParams(
            collective_id=0, has_side_effects=True, vmem_limit_bytes=60 * 2**20
        ),
    )(
        teacher_hidden,
        jnp.swapaxes(teacher_weight, 1, 2),
        student_hidden,
        student_weight.T,
        branch_weight[None],
        assignment[None],
        spread,
    )
    mine = lax.dynamic_slice(result, (0, first), (2, per))
    return mine[0], mine[1]


def solution(mesh):
    in_specs = (
        P("branch", None, "vocab"),
        P("branch", None, "vocab"),
        P("branch", "vocab"),
        P(None, "vocab"),
        P(),
        P(),
        P("branch"),
    )
    out_specs = (P("branch"), P("branch"))
    return jax.shard_map(
        per_device, mesh=mesh, in_specs=in_specs, out_specs=out_specs, check_vma=False
    )
```

```python
import functools

import jax
import jax.numpy as jnp
from jax import lax
from jax.experimental import pallas as pl
from jax.experimental.pallas import tpu as pltpu
from jax.sharding import PartitionSpec as P

MESH = pl.DeviceIdType.MESH
SCALE = 2.0**30
LOG_SCALE = 20.79441541679836
LANES = 128
PIECES = 10
BLOCK = 80
TILE = 800
SLOTS = 4
LAG = 2


def divisor(width, most):
    return max(t for t in range(8, most + 1, 8) if width % t == 0)


def piece_rows(width):
    return min(t for t in range(8, width + 1, 8) if width % t == 0 and width // t <= PIECES)


def flip(chip, e, chips):
    out, bit = 0, 1
    while bit < chips:
        out = out + bit * ((chip // bit + e // bit) % 2)
        bit *= 2
    return out


def kernel(
    n, nv, hidden, weight, student, s_weight, branch_weight, assignment, targets, out,
    hid, shid, wbuf, acc, sacc, up_in, down_in, up_out, down_out, factor, s_top, rows_in, fin_in, tbuf, res,
    local_sem, w_sem, h_send, h_recv, s_send, s_recv, p_send, p_recv, t_send, t_recv,
    up_send, up_recv, down_send, down_recv, l_send, l_recv, f_send, f_recv, r_send, r_recv,
):
    z, v = lax.axis_index("branch"), lax.axis_index("vocab")
    chips = nv // 2
    chip, core = v // 2, v % 2
    sibling = v + 1 - 2 * core
    half_n = n // 2
    batches, feat = hid.shape[0], hid.shape[3]
    tokens = batches * 2 * LANES
    half, per, width = tokens // 2, tokens // n, acc.shape[1]
    rows_each = piece_rows(width)
    pieces = width // rows_each
    block, tile_rows = divisor(width, BLOCK), divisor(width, TILE)
    upper = z // half_n
    end = upper * (n - 1)
    is_end = z == end
    place = z % half_n

    def remote(src, dst, send, recv, zz, vv):
        return pltpu.make_async_remote_copy(
            src_ref=src, dst_ref=dst, send_sem=send, recv_sem=recv, device_id=(zz, vv), device_id_type=MESH
        )

    def owner(s):
        return flip(chip, s // 2, chips) * 2 + (core + s) % 2

    def fetch(src, q):
        s, slot = q % nv, q % SLOTS
        features = pl.ds(pl.multiple_of(owner(s) * feat, feat), feat)
        return pltpu.make_async_copy(src.at[:, features], wbuf.at[slot], w_sem.at[slot])

    def prefetch(q):
        @pl.when(q < batches * nv)
        def _():
            fetch(t_weight, q).start()

        @pl.when(is_end & (q >= batches * nv) & (q < (batches + 1) * nv))
        def _():
            fetch(s_weight, q).start()

    t_weight = weight.at[0]
    own = []
    for b in range(batches):
        for side in range(2):
            own.append(pltpu.make_async_copy(
                hidden.at[0, pl.ds(side * half + b * LANES, LANES)],
                hid.at[b, 0, pl.ds(side * LANES, LANES)],
                local_sem.at[2 + 2 * b + side],
            ))
            own[-1].start()
    mine = pl.ds(pl.multiple_of(place * per, per), per)
    own_student = pltpu.make_async_copy(student, shid.at[0, mine], local_sem.at[0])
    own_targets = pltpu.make_async_copy(targets, tbuf.at[place], local_sem.at[1])

    @pl.when(is_end)
    def _():
        own_student.start()
        own_targets.start()

    for q in range(SLOTS - 1):
        fetch(t_weight, q).start()

    def block_rows(i):
        return pl.ds(pl.multiple_of(i * block, block), block)

    def clear(b):
        @pl.loop(0, width // block)
        def _(i):
            acc[b, block_rows(i), :] = jnp.zeros((block, 2 * LANES), jnp.float32)

    barrier = pltpu.get_barrier_semaphore()
    for d in range(1, nv):
        pl.semaphore_signal(barrier, inc=1, device_id=(z, (v + d) % nv), device_id_type=MESH)
    for d in range(1, n):
        pl.semaphore_signal(barrier, inc=1, device_id=((z + d) % n, v), device_id_type=MESH)
    clear(0)
    for copy in own:
        copy.wait()
    pl.semaphore_wait(barrier, nv - 1 + n - 1)

    def push(buf, send, recv, e):
        return remote(buf.at[0], buf.at[2 * e], send.at[2 * e], recv.at[2 * e], z, flip(chip, e, chips) * 2 + core)

    def forward(buf, send, recv, e):
        return remote(buf.at[2 * e], buf.at[2 * e + 1], send.at[2 * e + 1], recv.at[2 * e + 1], z, sibling)

    def begin(buf, send, recv):
        forward(buf, send, recv, 0).start()
        for e in range(1, min(3, chips)):
            push(buf, send, recv, e).start()

    def chunk_step(q, buf, send, recv, total, then):
        s, slot = q % nv, q % SLOTS
        e = s // 2
        prefetch(q + SLOTS - 1)

        @pl.when((s % 2 == 0) & (s > 0))
        def _():
            push(buf, send, recv, e).wait_recv()
            forward(buf, send, recv, e).start()

            @pl.when(e + 2 < chips)
            def _():
                push(buf, send, recv, e + 2).start()

            @pl.when(e == chips - 1)
            def _():
                then()

        @pl.when(s % 2 == 1)
        def _():
            forward(buf, send, recv, e).wait_recv()

        fetch(t_weight, q).wait()

        @pl.loop(0, width // tile_rows)
        def _(j):
            rows = pl.ds(pl.multiple_of(j * tile_rows, tile_rows), tile_rows)
            total[rows, :] += lax.dot_general(
                wbuf[slot, rows, :], buf[s], (((1,), (1,)), ((), ())), preferred_element_type=jnp.float32
            )

    def finish_sends(buf, send, recv):
        @pl.loop(0, chips)
        def _(e):
            forward(buf, send, recv, e).wait_send()

        @pl.loop(1, chips)
        def _(e):
            push(buf, send, recv, e).wait_send()

    def of_batch(b):
        return hid.at[b], h_send.at[b], h_recv.at[b]

    begin(*of_batch(0))

    pass_student = remote(student, shid.at[0, mine], p_send, p_recv.at[place], end, v)
    pass_targets = remote(targets, tbuf.at[place], t_send, t_recv.at[place], end, v)

    @pl.when(z != end)
    def _():
        pass_student.start()
        pass_targets.start()

    for b in range(1, batches):
        clear(b)

    @pl.when(is_end)
    def _():
        @pl.loop(0, width // block)
        def _(i):
            sacc[block_rows(i), :] = jnp.zeros((block, half), jnp.float32)

    def begin_student():
        @pl.when(is_end)
        def _():
            own_student.wait()
            own_targets.wait()

            @pl.loop(0, half_n)
            def _(j):
                @pl.when(j != place)
                def _():
                    there = pl.ds(pl.multiple_of(j * per, per), per)
                    remote(student, shid.at[0, there], p_send, p_recv.at[j], z, v).wait_recv()
                    remote(targets, tbuf.at[j], t_send, t_recv.at[j], z, v).wait_recv()

            begin(shid, s_send, s_recv)

    def teacher_step(b, s):
        def then():
            @pl.when(b + 1 < batches)
            def _():
                begin(*of_batch(b + 1))

            @pl.when(b + 1 == batches)
            def _():
                begin_student()

        chunk_step(b * nv + s, *of_batch(b), acc.at[b], then)

    def fold(x, reduce):
        return reduce(x.reshape(block // 8, 8, x.shape[1]), axis=0)

    def highest(logits):
        low = jnp.full((8, logits.shape[1]), -jnp.inf, jnp.float32)
        top = lax.fori_loop(
            0, width // block, lambda i, top: jnp.maximum(top, fold(logits[block_rows(i), :], jnp.max)), low
        )
        return jnp.max(top, axis=0, keepdims=True)

    def rows_of(*values):
        row = lax.broadcasted_iota(jnp.int32, (8, values[0].shape[1]), 0)
        packed = jnp.zeros(row.shape, jnp.float32)
        for i, value in enumerate(values):
            packed = jnp.where(row == i, value, packed)
        return packed

    def normalize(b):
        logits = acc.at[b]
        top = highest(logits)

        def exponentials(i, total):
            x = jnp.exp(logits[block_rows(i), :] - top)
            logits[block_rows(i), :] = x
            return total + fold(x, jnp.sum)

        total = lax.fori_loop(0, width // block, exponentials, jnp.zeros((8, 2 * LANES), jnp.float32))
        rows_in[b, 0] = rows_of(top, jnp.sum(total, axis=0, keepdims=True))
        exchange_start(rows_in.at[b], l_send.at[b], l_recv.at[b])

    def exchange_start(buf, send, recv):
        @pl.loop(1, nv)
        def _(d):
            remote(buf.at[0], buf.at[d], send.at[d], recv.at[d], z, (v + d) % nv).start()

    def exchange_wait(buf, send, recv):
        @pl.loop(1, nv)
        def _(d):
            remote(buf.at[0], buf.at[d], send.at[d], recv.at[d], z, (v + d) % nv).wait()

    def merge(buf):
        top = buf[0, 0:1, :]
        for d in range(1, nv):
            top = jnp.maximum(top, buf[d, 0:1, :])
        total = jnp.zeros_like(top)
        for d in range(nv):
            total += buf[d, 1:2, :] * jnp.exp(buf[d, 0:1, :] - top)
        return top + jnp.log(total)

    weights = branch_weight[...]
    log_share = jnp.log(weights / jnp.sum(weights, axis=1, keepdims=True))
    index = lax.broadcasted_iota(jnp.int32, weights.shape, 1)
    chosen = jnp.sum(
        jnp.where(index == z, assignment[...].astype(jnp.float32), 0.0), axis=1, keepdims=True
    )
    own_share = jnp.sum(
        jnp.where(index.astype(jnp.float32) == chosen, log_share, 0.0), axis=1, keepdims=True
    )
    def weigh(b):
        stats = rows_in.at[b]
        exchange_wait(stats, l_send.at[b], l_recv.at[b])
        scale = jnp.exp(stats[0, 0:1, :] - merge(stats) + own_share) * SCALE
        factor[b] = jnp.broadcast_to(scale, (8, 2 * LANES))

    @pl.loop(0, nv)
    def _(s):
        teacher_step(0, s)

    normalize(0)

    def piece_up(c):
        return remote(up_out.at[c], up_in.at[c], up_send.at[c], up_recv.at[c], lax.rem(z + 1, n), v)

    def piece_down(c):
        return remote(down_out.at[c], down_in.at[c], down_send.at[c], down_recv.at[c], lax.rem(z + n - 1, n), v)

    def turn(c, side, order, piece, came, leaves):
        b = c // pieces
        rows = pl.ds(pl.multiple_of(c % pieces * rows_each, rows_each), rows_each)
        lanes = pl.ds(side * LANES, LANES)

        @pl.when(order == 0)
        def _():
            p = acc[b, rows, lanes] * factor[b, :1, lanes]
            p = p * p
            leaves[c] = (p * p).astype(jnp.bfloat16)
            piece(c).start()

        @pl.when(order > 0)
        def _():
            piece(c).wait_recv()
            p = acc[b, rows, lanes] * factor[b, :1, lanes] + lax.rsqrt(lax.rsqrt(came[c].astype(jnp.float32)))

            @pl.when(order < n - 1)
            def _():
                square = p * p
                leaves[c] = (square * square).astype(jnp.bfloat16)
                piece(c).start()

            @pl.when(order == n - 1)
            def _():
                acc[b, rows, lanes] = p

    def find_top():
        s_top[...] = jnp.broadcast_to(highest(sacc), (8, half))

    def compare(b):
        lanes = pl.ds(pl.multiple_of(upper * LANES, LANES), LANES)
        here = pl.ds(b * LANES, LANES)
        top = s_top[:1, here]
        picks = tbuf[0, :1, here]
        for j in range(1, half_n):
            picks = picks + tbuf[j, :1, here]
        picks = picks - v * width
        vocab_row = lax.broadcasted_iota(jnp.int32, (block, LANES), 0)

        def terms(i, sums):
            x = sacc[block_rows(i), here]
            q = acc[b, block_rows(i), lanes]
            hit = jnp.where(vocab_row + i * block == picks, x, 0.0)
            x = x - top
            mixture = jnp.log(jnp.maximum(q, 1e-30)) - LOG_SCALE
            q = q * (1.0 / SCALE)
            new = (jnp.exp(x), hit, q * (mixture - x), q)
            return tuple(old + fold(value, jnp.sum) for old, value in zip(sums, new))

        sums = lax.fori_loop(0, width // block, terms, (jnp.zeros((8, LANES), jnp.float32),) * 4)
        fin_in[0, :, here] = rows_of(top, *(jnp.sum(value, axis=0, keepdims=True) for value in sums))

    busy = pieces - 2
    each = -(-nv // busy)

    @pl.loop(0, batches * pieces + LAG * (n - 1))
    def _(k):
        period, j = k // pieces, k % pieces

        @pl.when((j == 0) & (period < batches))
        def _():
            weigh(period)

        c = k - LAG * z

        @pl.when((c >= 0) & (c < batches * pieces))
        def _():
            turn(c, 1, z, piece_up, up_in, up_out)

        o = n - 1 - z
        d = k - LAG * o

        @pl.when((d >= 0) & (d < batches * pieces))
        def _():
            turn(d, 0, o, piece_down, down_in, down_out)

        @pl.when((period + 1 < batches) & (j < busy))
        def _():
            for u in range(each):
                @pl.when(j * each + u < nv)
                def _():
                    teacher_step(period + 1, j * each + u)

        @pl.when((period + 1 < batches) & (j == busy))
        def _():
            normalize(period + 1)

        @pl.when(is_end & (period + 1 == batches) & (j < busy))
        def _():
            for u in range(each):
                @pl.when(j * each + u < nv)
                def _():
                    chunk_step(batches * nv + j * each + u, shid, s_send, s_recv, sacc, lambda: None)

        @pl.when(is_end & (period + 1 == batches) & (j == busy))
        def _():
            find_top()

        for b in range(batches - 1):
            ready = max(batches * pieces - 1 + b, (b + 1) * pieces + LAG * (n - 1))

            @pl.when(is_end & (k == ready))
            def _():
                compare(b)

    @pl.when(is_end)
    def _():
        compare(batches - 1)
        exchange_start(fin_in, f_send, f_recv)
        exchange_wait(fin_in, f_send, f_recv)
        lse = merge(fin_in)
        hit, cross, mass = (jnp.zeros((1, half), jnp.float32) for _ in range(3))
        for d in range(nv):
            hit += fin_in[d, 2:3, :]
            mass += fin_in[d, 4:5, :]
            cross += fin_in[d, 3:4, :] + fin_in[d, 4:5, :] * (lse - fin_in[d, 0:1, :])
        row = lax.broadcasted_iota(jnp.int32, (8, half), 0)
        res[...] = jnp.where(row == 0, cross / mass - jnp.log(mass), lse - hit)

        def give(j):
            return remote(res, res, r_send.at[j], r_recv, upper * half_n + j, v)

        for act in ("start", "wait_send"):
            @pl.loop(0, half_n)
            def _(j):
                @pl.when(j != place)
                def _():
                    getattr(give(j), act)()

        finish_sends(shid, s_send, s_recv)

    @pl.when(z != end)
    def _():
        remote(res, res, r_send.at[0], r_recv, end, v).wait_recv()
        pass_student.wait_send()
        pass_targets.wait_send()

    out[...] = res[...]
    for b in range(batches):
        finish_sends(*of_batch(b))

    @pl.loop(0, batches * pieces)
    def _(c):
        @pl.when(z < n - 1)
        def _():
            piece_up(c).wait_send()

        @pl.when(z > 0)
        def _():
            piece_down(c).wait_send()


def per_device(
    teacher_hidden,
    teacher_weight,
    student_hidden,
    student_weight,
    branch_weight,
    assignment,
    targets,
):
    n, nv = lax.axis_size("branch"), lax.axis_size("vocab")
    _, tokens, feat = teacher_hidden.shape
    width = teacher_weight.shape[2]
    half, per = tokens // 2, tokens // n
    rows_each = piece_rows(width)
    batches = half // LANES
    moves = batches * (width // rows_each)
    first = lax.axis_index("branch") % (n // 2) * per
    spread = jnp.zeros((8, half), jnp.int32)
    spread = lax.dynamic_update_slice(spread, jnp.broadcast_to(targets[None], (8, per)), (0, first))
    f32, bf16 = jnp.float32, jnp.bfloat16
    dma = pltpu.SemaphoreType.DMA
    anywhere = pl.BlockSpec(memory_space=pl.ANY)
    vmem = pl.BlockSpec(memory_space=pltpu.VMEM)
    result = pl.pallas_call(
        functools.partial(kernel, n, nv),
        out_shape=jax.ShapeDtypeStruct((8, half), f32),
        in_specs=[anywhere, anywhere, anywhere, anywhere, vmem, vmem, vmem],
        out_specs=vmem,
        scratch_shapes=[
            pltpu.VMEM((batches, nv, 2 * LANES, feat), bf16),
            pltpu.VMEM((nv, half, feat), bf16),
            pltpu.VMEM((SLOTS, width, feat), bf16),
            pltpu.VMEM((batches, width, 2 * LANES), f32),
            pltpu.VMEM((width, half), f32),
            pltpu.VMEM((moves, rows_each, LANES), bf16),
            pltpu.VMEM((moves, rows_each, LANES), bf16),
            pltpu.VMEM((moves, rows_each, LANES), bf16),
            pltpu.VMEM((moves, rows_each, LANES), bf16),
            pltpu.VMEM((batches, 8, 2 * LANES), f32),
            pltpu.VMEM((8, half), f32),
            pltpu.VMEM((batches, nv, 8, 2 * LANES), f32),
            pltpu.VMEM((nv, 8, half), f32),
            pltpu.VMEM((n // 2, 8, half), jnp.int32),
            pltpu.VMEM((8, half), f32),
            dma((2 + 2 * batches,)),
            dma((SLOTS,)),
            dma((batches, nv)), dma((batches, nv)),
            dma((nv,)), dma((nv,)),
            dma, dma((n // 2,)),
            dma, dma((n // 2,)),
            dma((moves,)), dma((moves,)),
            dma((moves,)), dma((moves,)),
            dma((batches, nv)), dma((batches, nv)),
            dma((nv,)), dma((nv,)),
            dma((n // 2,)), dma,
        ],
        compiler_params=pltpu.CompilerParams(
            collective_id=0, has_side_effects=True, vmem_limit_bytes=60 * 2**20
        ),
    )(
        teacher_hidden,
        jnp.swapaxes(teacher_weight, 1, 2),
        student_hidden,
        student_weight.T,
        branch_weight[None],
        assignment[None],
        spread,
    )
    mine = lax.dynamic_slice(result, (0, first), (2, per))
    return mine[0], mine[1]


def solution(mesh):
    in_specs = (
        P("branch", None, "vocab"),
        P("branch", None, "vocab"),
        P("branch", "vocab"),
        P(None, "vocab"),
        P(),
        P(),
        P("branch"),
    )
    out_specs = (P("branch"), P("branch"))
    return jax.shard_map(
        per_device, mesh=mesh, in_specs=in_specs, out_specs=out_specs, check_vma=False
    )
```

```python
import functools

import jax
import jax.numpy as jnp
from jax import lax
from jax.experimental import pallas as pl
from jax.experimental.pallas import tpu as pltpu
from jax.sharding import PartitionSpec as P

MESH = pl.DeviceIdType.MESH
SCALE = 2.0**30
LOG_SCALE = 20.79441541679836
LANES = 128
PIECES = 10
BLOCK = 80
TILE = 2000
SLOTS = 4
LAG = 2


def divisor(width, most):
    return max(t for t in range(8, most + 1, 8) if width % t == 0)


def piece_rows(width):
    return min(t for t in range(8, width + 1, 8) if width % t == 0 and width // t <= PIECES)


def flip(chip, e, chips):
    out, bit = 0, 1
    while bit < chips:
        out = out + bit * ((chip // bit + e // bit) % 2)
        bit *= 2
    return out


def kernel(
    n, nv, hidden, weight, student, s_weight, branch_weight, assignment, targets, out,
    hid, shid, wbuf, acc, sacc, up_in, down_in, up_out, down_out, factor, s_top, rows_in, fin_in, tbuf, res,
    local_sem, w_sem, h_send, h_recv, s_send, s_recv, p_send, p_recv, t_send, t_recv,
    up_send, up_recv, down_send, down_recv, l_send, l_recv, f_send, f_recv, r_send, r_recv,
):
    z, v = lax.axis_index("branch"), lax.axis_index("vocab")
    chips = nv // 2
    chip, core = v // 2, v % 2
    sibling = v + 1 - 2 * core
    half_n = n // 2
    batches, feat = hid.shape[0], hid.shape[3]
    tokens = batches * 2 * LANES
    half, per, width = tokens // 2, tokens // n, acc.shape[1]
    rows_each = piece_rows(width)
    pieces = width // rows_each
    block, tile_rows = divisor(width, BLOCK), divisor(width, TILE)
    upper = z // half_n
    end = upper * (n - 1)
    is_end = z == end
    place = z % half_n

    def remote(src, dst, send, recv, zz, vv):
        return pltpu.make_async_remote_copy(
            src_ref=src, dst_ref=dst, send_sem=send, recv_sem=recv, device_id=(zz, vv), device_id_type=MESH
        )

    def owner(s):
        return flip(chip, s // 2, chips) * 2 + (core + s) % 2

    def fetch(src, q):
        s, slot = q % nv, q % SLOTS
        features = pl.ds(pl.multiple_of(owner(s) * feat, feat), feat)
        return pltpu.make_async_copy(src.at[:, features], wbuf.at[slot], w_sem.at[slot])

    def prefetch(q):
        @pl.when(q < batches * nv)
        def _():
            fetch(t_weight, q).start()

        @pl.when(is_end & (q >= batches * nv) & (q < (batches + 1) * nv))
        def _():
            fetch(s_weight, q).start()

    t_weight = weight.at[0]
    own = []
    for b in range(batches):
        for side in range(2):
            own.append(pltpu.make_async_copy(
                hidden.at[0, pl.ds(side * half + b * LANES, LANES)],
                hid.at[b, 0, pl.ds(side * LANES, LANES)],
                local_sem.at[2 + 2 * b + side],
            ))
            own[-1].start()
    mine = pl.ds(pl.multiple_of(place * per, per), per)
    own_student = pltpu.make_async_copy(student, shid.at[0, mine], local_sem.at[0])
    own_targets = pltpu.make_async_copy(targets, tbuf.at[place], local_sem.at[1])

    @pl.when(is_end)
    def _():
        own_student.start()
        own_targets.start()

    for q in range(SLOTS - 1):
        fetch(t_weight, q).start()

    def block_rows(i):
        return pl.ds(pl.multiple_of(i * block, block), block)

    def clear(b):
        @pl.loop(0, width // block)
        def _(i):
            acc[b, block_rows(i), :] = jnp.zeros((block, 2 * LANES), jnp.float32)

    barrier = pltpu.get_barrier_semaphore()
    for d in range(1, nv):
        pl.semaphore_signal(barrier, inc=1, device_id=(z, (v + d) % nv), device_id_type=MESH)
    for d in range(1, n):
        pl.semaphore_signal(barrier, inc=1, device_id=((z + d) % n, v), device_id_type=MESH)
    clear(0)
    for copy in own:
        copy.wait()
    pl.semaphore_wait(barrier, nv - 1 + n - 1)

    def push(buf, send, recv, e):
        return remote(buf.at[0], buf.at[2 * e], send.at[2 * e], recv.at[2 * e], z, flip(chip, e, chips) * 2 + core)

    def forward(buf, send, recv, e):
        return remote(buf.at[2 * e], buf.at[2 * e + 1], send.at[2 * e + 1], recv.at[2 * e + 1], z, sibling)

    def begin(buf, send, recv):
        forward(buf, send, recv, 0).start()
        for e in range(1, min(3, chips)):
            push(buf, send, recv, e).start()

    def chunk_step(q, buf, send, recv, total, then):
        s, slot = q % nv, q % SLOTS
        e = s // 2
        prefetch(q + SLOTS - 1)

        @pl.when((s % 2 == 0) & (s > 0))
        def _():
            push(buf, send, recv, e).wait_recv()
            forward(buf, send, recv, e).start()

            @pl.when(e + 2 < chips)
            def _():
                push(buf, send, recv, e + 2).start()

            @pl.when(e == chips - 1)
            def _():
                then()

        @pl.when(s % 2 == 1)
        def _():
            forward(buf, send, recv, e).wait_recv()

        fetch(t_weight, q).wait()

        @pl.loop(0, width // tile_rows)
        def _(j):
            rows = pl.ds(pl.multiple_of(j * tile_rows, tile_rows), tile_rows)
            total[rows, :] += lax.dot_general(
                wbuf[slot, rows, :], buf[s], (((1,), (1,)), ((), ())), preferred_element_type=jnp.float32
            )

    def finish_sends(buf, send, recv):
        @pl.loop(0, chips)
        def _(e):
            forward(buf, send, recv, e).wait_send()

        @pl.loop(1, chips)
        def _(e):
            push(buf, send, recv, e).wait_send()

    def of_batch(b):
        return hid.at[b], h_send.at[b], h_recv.at[b]

    begin(*of_batch(0))

    pass_student = remote(student, shid.at[0, mine], p_send, p_recv.at[place], end, v)
    pass_targets = remote(targets, tbuf.at[place], t_send, t_recv.at[place], end, v)

    @pl.when(z != end)
    def _():
        pass_student.start()
        pass_targets.start()

    for b in range(1, batches):
        clear(b)

    @pl.when(is_end)
    def _():
        @pl.loop(0, width // block)
        def _(i):
            sacc[block_rows(i), :] = jnp.zeros((block, half), jnp.float32)

    def begin_student():
        @pl.when(is_end)
        def _():
            own_student.wait()
            own_targets.wait()

            @pl.loop(0, half_n)
            def _(j):
                @pl.when(j != place)
                def _():
                    there = pl.ds(pl.multiple_of(j * per, per), per)
                    remote(student, shid.at[0, there], p_send, p_recv.at[j], z, v).wait_recv()
                    remote(targets, tbuf.at[j], t_send, t_recv.at[j], z, v).wait_recv()

            begin(shid, s_send, s_recv)

    def teacher_step(b, s):
        def then():
            @pl.when(b + 1 < batches)
            def _():
                begin(*of_batch(b + 1))

            @pl.when(b + 1 == batches)
            def _():
                begin_student()

        chunk_step(b * nv + s, *of_batch(b), acc.at[b], then)

    def fold(x, reduce):
        return reduce(x.reshape(block // 8, 8, x.shape[1]), axis=0)

    def highest(logits):
        low = jnp.full((8, logits.shape[1]), -jnp.inf, jnp.float32)
        top = lax.fori_loop(
            0, width // block, lambda i, top: jnp.maximum(top, fold(logits[block_rows(i), :], jnp.max)), low
        )
        return jnp.max(top, axis=0, keepdims=True)

    def rows_of(*values):
        row = lax.broadcasted_iota(jnp.int32, (8, values[0].shape[1]), 0)
        packed = jnp.zeros(row.shape, jnp.float32)
        for i, value in enumerate(values):
            packed = jnp.where(row == i, value, packed)
        return packed

    def normalize(b):
        logits = acc.at[b]
        top = highest(logits)

        def exponentials(i, total):
            x = jnp.exp(logits[block_rows(i), :] - top)
            logits[block_rows(i), :] = x
            return total + fold(x, jnp.sum)

        total = lax.fori_loop(0, width // block, exponentials, jnp.zeros((8, 2 * LANES), jnp.float32))
        rows_in[b, 0] = rows_of(top, jnp.sum(total, axis=0, keepdims=True))
        exchange_start(rows_in.at[b], l_send.at[b], l_recv.at[b])

    def exchange_start(buf, send, recv):
        @pl.loop(1, nv)
        def _(d):
            remote(buf.at[0], buf.at[d], send.at[d], recv.at[d], z, (v + d) % nv).start()

    def exchange_wait(buf, send, recv):
        @pl.loop(1, nv)
        def _(d):
            remote(buf.at[0], buf.at[d], send.at[d], recv.at[d], z, (v + d) % nv).wait()

    def merge(buf):
        top = buf[0, 0:1, :]
        for d in range(1, nv):
            top = jnp.maximum(top, buf[d, 0:1, :])
        total = jnp.zeros_like(top)
        for d in range(nv):
            total += buf[d, 1:2, :] * jnp.exp(buf[d, 0:1, :] - top)
        return top + jnp.log(total)

    weights = branch_weight[...]
    log_share = jnp.log(weights / jnp.sum(weights, axis=1, keepdims=True))
    index = lax.broadcasted_iota(jnp.int32, weights.shape, 1)
    chosen = jnp.sum(
        jnp.where(index == z, assignment[...].astype(jnp.float32), 0.0), axis=1, keepdims=True
    )
    own_share = jnp.sum(
        jnp.where(index.astype(jnp.float32) == chosen, log_share, 0.0), axis=1, keepdims=True
    )
    def weigh(b):
        stats = rows_in.at[b]
        exchange_wait(stats, l_send.at[b], l_recv.at[b])
        scale = jnp.exp(stats[0, 0:1, :] - merge(stats) + own_share) * SCALE
        factor[b] = jnp.broadcast_to(scale, (8, 2 * LANES))

    @pl.loop(0, nv)
    def _(s):
        teacher_step(0, s)

    normalize(0)

    def piece_up(c):
        return remote(up_out.at[c], up_in.at[c], up_send.at[c], up_recv.at[c], lax.rem(z + 1, n), v)

    def piece_down(c):
        return remote(down_out.at[c], down_in.at[c], down_send.at[c], down_recv.at[c], lax.rem(z + n - 1, n), v)

    def turn(c, side, order, piece, came, leaves):
        b = c // pieces
        rows = pl.ds(pl.multiple_of(c % pieces * rows_each, rows_each), rows_each)
        lanes = pl.ds(side * LANES, LANES)

        @pl.when(order == 0)
        def _():
            p = acc[b, rows, lanes] * factor[b, :1, lanes]
            p = p * p
            leaves[c] = (p * p).astype(jnp.bfloat16)
            piece(c).start()

        @pl.when(order > 0)
        def _():
            piece(c).wait_recv()
            p = acc[b, rows, lanes] * factor[b, :1, lanes] + lax.rsqrt(lax.rsqrt(came[c].astype(jnp.float32)))

            @pl.when(order < n - 1)
            def _():
                square = p * p
                leaves[c] = (square * square).astype(jnp.bfloat16)
                piece(c).start()

            @pl.when(order == n - 1)
            def _():
                acc[b, rows, lanes] = p

    def find_top():
        s_top[...] = jnp.broadcast_to(highest(sacc), (8, half))

    def compare(b):
        lanes = pl.ds(pl.multiple_of(upper * LANES, LANES), LANES)
        here = pl.ds(b * LANES, LANES)
        top = s_top[:1, here]
        picks = tbuf[0, :1, here]
        for j in range(1, half_n):
            picks = picks + tbuf[j, :1, here]
        picks = picks - v * width
        vocab_row = lax.broadcasted_iota(jnp.int32, (block, LANES), 0)

        def terms(i, sums):
            x = sacc[block_rows(i), here]
            q = acc[b, block_rows(i), lanes]
            hit = jnp.where(vocab_row + i * block == picks, x, 0.0)
            x = x - top
            mixture = jnp.log(jnp.maximum(q, 1e-30)) - LOG_SCALE
            q = q * (1.0 / SCALE)
            new = (jnp.exp(x), hit, q * (mixture - x), q)
            return tuple(old + fold(value, jnp.sum) for old, value in zip(sums, new))

        sums = lax.fori_loop(0, width // block, terms, (jnp.zeros((8, LANES), jnp.float32),) * 4)
        fin_in[0, :, here] = rows_of(top, *(jnp.sum(value, axis=0, keepdims=True) for value in sums))

    busy = pieces - 2
    each = -(-nv // busy)

    @pl.loop(0, batches * pieces + LAG * (n - 1))
    def _(k):
        period, j = k // pieces, k % pieces

        @pl.when((j == 0) & (period < batches))
        def _():
            weigh(period)

        ahead = k - (batches - 1) * pieces

        def turns(side, order, *rest):
            c = k - LAG * order

            @pl.when((c >= 0) & (c < batches * pieces) & ((order > 0) | (ahead <= 0)))
            def _():
                turn(c, side, order, *rest)

            @pl.when((order == 0) & (ahead > 0))
            def _():
                for u in range(2):
                    later = (batches - 1) * pieces + 2 * ahead - 1 + u

                    @pl.when(later < batches * pieces)
                    def _():
                        turn(later, side, order, *rest)

        turns(1, z, piece_up, up_in, up_out)
        turns(0, n - 1 - z, piece_down, down_in, down_out)

        @pl.when((period + 1 < batches) & (j < busy))
        def _():
            @pl.loop(0, each)
            def _(u):
                @pl.when(j * each + u < nv)
                def _():
                    teacher_step(period + 1, j * each + u)

        @pl.when((period + 1 < batches) & (j == busy))
        def _():
            normalize(period + 1)

        @pl.when(is_end & (period + 1 == batches) & (j < busy))
        def _():
            @pl.loop(0, each)
            def _(u):
                @pl.when(j * each + u < nv)
                def _():
                    chunk_step(batches * nv + j * each + u, shid, s_send, s_recv, sacc, lambda: None)

        @pl.when(is_end & (period + 1 == batches) & (j == busy))
        def _():
            find_top()

        for b in range(batches - 1):
            ready = max(batches * pieces - 1 + b, (b + 1) * pieces + LAG * (n - 1))

            @pl.when(is_end & (k == ready))
            def _():
                compare(b)

    @pl.when(is_end)
    def _():
        compare(batches - 1)
        exchange_start(fin_in, f_send, f_recv)
        exchange_wait(fin_in, f_send, f_recv)
        lse = merge(fin_in)
        hit, cross, mass = (jnp.zeros((1, half), jnp.float32) for _ in range(3))
        for d in range(nv):
            hit += fin_in[d, 2:3, :]
            mass += fin_in[d, 4:5, :]
            cross += fin_in[d, 3:4, :] + fin_in[d, 4:5, :] * (lse - fin_in[d, 0:1, :])
        row = lax.broadcasted_iota(jnp.int32, (8, half), 0)
        res[...] = jnp.where(row == 0, cross / mass - jnp.log(mass), lse - hit)

        def give(j):
            return remote(res, res, r_send.at[j], r_recv, upper * half_n + j, v)

        for act in ("start", "wait_send"):
            @pl.loop(0, half_n)
            def _(j):
                @pl.when(j != place)
                def _():
                    getattr(give(j), act)()

        finish_sends(shid, s_send, s_recv)

    @pl.when(z != end)
    def _():
        remote(res, res, r_send.at[0], r_recv, end, v).wait_recv()
        pass_student.wait_send()
        pass_targets.wait_send()

    out[...] = res[...]
    for b in range(batches):
        finish_sends(*of_batch(b))

    @pl.loop(0, batches * pieces)
    def _(c):
        @pl.when(z < n - 1)
        def _():
            piece_up(c).wait_send()

        @pl.when(z > 0)
        def _():
            piece_down(c).wait_send()


def per_device(
    teacher_hidden,
    teacher_weight,
    student_hidden,
    student_weight,
    branch_weight,
    assignment,
    targets,
):
    n, nv = lax.axis_size("branch"), lax.axis_size("vocab")
    _, tokens, feat = teacher_hidden.shape
    width = teacher_weight.shape[2]
    half, per = tokens // 2, tokens // n
    rows_each = piece_rows(width)
    batches = half // LANES
    moves = batches * (width // rows_each)
    first = lax.axis_index("branch") % (n // 2) * per
    spread = jnp.zeros((8, half), jnp.int32)
    spread = lax.dynamic_update_slice(spread, jnp.broadcast_to(targets[None], (8, per)), (0, first))
    f32, bf16 = jnp.float32, jnp.bfloat16
    dma = pltpu.SemaphoreType.DMA
    anywhere = pl.BlockSpec(memory_space=pl.ANY)
    vmem = pl.BlockSpec(memory_space=pltpu.VMEM)
    result = pl.pallas_call(
        functools.partial(kernel, n, nv),
        out_shape=jax.ShapeDtypeStruct((8, half), f32),
        in_specs=[anywhere, anywhere, anywhere, anywhere, vmem, vmem, vmem],
        out_specs=vmem,
        scratch_shapes=[
            pltpu.VMEM((batches, nv, 2 * LANES, feat), bf16),
            pltpu.VMEM((nv, half, feat), bf16),
            pltpu.VMEM((SLOTS, width, feat), bf16),
            pltpu.VMEM((batches, width, 2 * LANES), f32),
            pltpu.VMEM((width, half), f32),
            pltpu.VMEM((moves, rows_each, LANES), bf16),
            pltpu.VMEM((moves, rows_each, LANES), bf16),
            pltpu.VMEM((moves, rows_each, LANES), bf16),
            pltpu.VMEM((moves, rows_each, LANES), bf16),
            pltpu.VMEM((batches, 8, 2 * LANES), f32),
            pltpu.VMEM((8, half), f32),
            pltpu.VMEM((batches, nv, 8, 2 * LANES), f32),
            pltpu.VMEM((nv, 8, half), f32),
            pltpu.VMEM((n // 2, 8, half), jnp.int32),
            pltpu.VMEM((8, half), f32),
            dma((2 + 2 * batches,)),
            dma((SLOTS,)),
            dma((batches, nv)), dma((batches, nv)),
            dma((nv,)), dma((nv,)),
            dma, dma((n // 2,)),
            dma, dma((n // 2,)),
            dma((moves,)), dma((moves,)),
            dma((moves,)), dma((moves,)),
            dma((batches, nv)), dma((batches, nv)),
            dma((nv,)), dma((nv,)),
            dma((n // 2,)), dma,
        ],
        compiler_params=pltpu.CompilerParams(
            collective_id=0, has_side_effects=True, vmem_limit_bytes=60 * 2**20
        ),
    )(
        teacher_hidden,
        jnp.swapaxes(teacher_weight, 1, 2),
        student_hidden,
        student_weight.T,
        branch_weight[None],
        assignment[None],
        spread,
    )
    mine = lax.dynamic_slice(result, (0, first), (2, per))
    return mine[0], mine[1]


def solution(mesh):
    in_specs = (
        P("branch", None, "vocab"),
        P("branch", None, "vocab"),
        P("branch", "vocab"),
        P(None, "vocab"),
        P(),
        P(),
        P("branch"),
    )
    out_specs = (P("branch"), P("branch"))
    return jax.shard_map(
        per_device, mesh=mesh, in_specs=in_specs, out_specs=out_specs, check_vma=False
    )
```
